256 devices in a mesh: dp: 64 (over y, z, core), mp: 4 (over x).
Axes of the slice: x: 4, y: 4, z: 8, core: 2. Of those that a mesh axis runs over, the one named last changes fastest.
Arguments:
- grads: bfloat16 [64, 256, 12288], P('dp', 'mp'), may hold values from -5 to 5
- master: float32 [256, 12288], P('mp', 'dp'), may hold values from -3 to 3
- moment: float32 [256, 12288], P('mp', 'dp'), may hold values from -0.6 to 0.6
- second: float32 [256, 12288], P('mp', 'dp'), may hold values from 0.003 to 0.3
- inputs: bfloat16 [32768, 12288], P(('dp', 'mp')), may hold values from -6 to 6
- out_grads: bfloat16 [32768, 1024], P('dp', 'mp'), may hold values from -0.26367188 to 0.26367188
Outputs:
- weights: bfloat16 [256, 12288], P('mp')
- new_master: float32 [256, 12288], P('mp', 'dp')
- new_moment: float32 [256, 12288], P('mp', 'dp')
- new_second: float32 [256, 12288], P('mp', 'dp')
- next_grads: bfloat16 [64, 1024, 12288], P('dp', 'mp')
The draws below stay inside these ranges and needn't reach their ends.
All inputs are finite; a program needn't handle non-finite values.
Results may differ from the reference program's by a relative error of at most 0.001.
Values may be sent and summed in bfloat16 or wider, within the bound.
No kernel may reach another device: no remote copies, remote signals or barrier semaphores. Data moves between devices by JAX's collectives and lax.ppermute only.
A program may use at most 128 MiB of HBM per device.

```python
import math
import jax
import jax.numpy as jnp
from jax import lax

D = 12288
TOK_DEV = 512
STEP = 10
ROWS_ALL = 256
NEXT_ALL = 1024
TOKENS = 32768
N_DP = 64


def raised(array, own_key, source, target, parts, factor):
    def block_of(axis_at):
        return (jnp.arange(array.shape[axis_at]) // (array.shape[axis_at] // parts)).reshape((-1,) + (1,) * (array.ndim - 1 - axis_at))

    one_side = jax.random.permutation(own_key, parts)[block_of(target)]
    second = (block_of(target) + parts // 2) % parts
    return jnp.where((block_of(source) == one_side) | (block_of(source) == second), factor * array, array)


def block_scale(key, extent, split, low, high):
    factor_of, own = 1.0, jax.random.fold_in(key, 6)
    for axis_at, shards_of in split:
        heights = jnp.exp(jax.random.uniform(jax.random.fold_in(own, axis_at), (shards_of,), jnp.float32, low / len(split), high / len(split)))
        factor_of = factor_of * jnp.repeat(heights, extent[axis_at] // shards_of).reshape([-1 if axis == axis_at else 1 for axis in range(len(extent))])
    return factor_of


def noise(rng, shape, scale, most, split=(), dtype=jnp.bfloat16):
    array = scale * jax.random.normal(rng, shape, jnp.float32)
    if split:
        array = array * block_scale(rng, shape, split, -0.22, 0.18)
    return jnp.clip(array, -most, most).astype(dtype)


def noise_with(own_key, dims, scale, limit, cuts, heavy, kind=jnp.bfloat16):
    entries = scale * jax.random.normal(own_key, dims, jnp.float32)
    if cuts:
        entries = entries * block_scale(own_key, dims, cuts, -0.22, 0.18)
    return jnp.clip(raised(entries, jax.random.fold_in(own_key, 3), *heavy), -limit, limit).astype(kind)


def setup_inputs(seed: int = 0) -> dict:
    streams_of = jax.random.split(jax.random.key(seed), 7)
    return {
        "grads": noise_with(streams_of[0], (N_DP, ROWS_ALL, D), (N_DP ** -0.5), 5.0, ((0, 64), (1, 4)), (0, 2, 64, 4.0)),
        "master": noise(streams_of[1], (ROWS_ALL, D), 0.5, 3.0, ((0, 4), (1, 64)), jnp.float32),
        "moment": noise(streams_of[2], (ROWS_ALL, D), 0.1, 0.6, ((0, 4), (1, 64)), jnp.float32),
        "second": jnp.clip(jnp.exp(math.log(0.3) - 4.6051702 * jax.random.uniform(streams_of[3], (ROWS_ALL, D), jnp.float32) ** block_scale(streams_of[3], (ROWS_ALL, D), ((0, 4), (1, 64)), -0.2, 0.2)), 0.003, 0.3),
        "inputs": noise(streams_of[4], (TOKENS, D), 1.0, 6.0, ((0, 256),)),
        "out_grads": noise(streams_of[5], (TOKENS, NEXT_ALL), (TOK_DEV ** -0.5), 0.26367188, ((0, 64), (1, 4))),
    }


beta_one = 0.9
beta_two = 0.95
learn_rate = 0.05
decay_rate = 0.1
adam_eps = 1e-08

def reference(grads, master, moment, second, inputs, out_grads):

    def add_replica(carry, piece):
        return (carry + piece.astype(jnp.float32), None)
    total, unused = lax.scan(add_replica, jnp.zeros(master.shape, jnp.float32), grads)
    new_moment = beta_one * moment + (1.0 - beta_one) * total
    new_second = beta_two * second + (1.0 - beta_two) * total * total
    first_hat = new_moment / (1.0 - beta_one ** STEP)
    second_hat = new_second / (1.0 - beta_two ** STEP)
    new_master = master - learn_rate * (first_hat / (jnp.sqrt(second_hat) + adam_eps) + decay_rate * master)
    weights = new_master.astype(jnp.bfloat16)
    split_inputs = inputs.reshape(N_DP, TOK_DEV, D)
    split_grads = out_grads.reshape(N_DP, TOK_DEV, NEXT_ALL)

    def replica_grad(pair):
        return jnp.dot(pair[1].T, pair[0], preferred_element_type=jnp.float32).astype(jnp.bfloat16)
    next_grads = lax.map(replica_grad, (split_inputs, split_grads))
    return (weights, new_master, new_moment, new_second, next_grads)
```

```python
import functools

import jax
import jax.numpy as jnp
from jax import lax
from jax.experimental import pallas as pl
from jax.experimental.pallas import tpu as pltpu
from jax.sharding import PartitionSpec as P

STEP = 10

beta_one = 0.9
beta_two = 0.95
learn_rate = 0.05
decay_rate = 0.1
adam_eps = 1e-08

NY, NZ, NC, NX = 4, 8, 2, 4
D = 12288
BLOCK = 1024
PIECES = ((0, 4096), (6144, 4096), (4096, 2048), (10240, 2048))


def dp_shift(dy, dz, dc):
    pairs = []
    for y in range(NY):
        for z in range(NZ):
            for c in range(NC):
                target = (((y + dy) % NY) * NZ + (z + dz) % NZ) * NC + (c + dc) % NC
                pairs.append(((y * NZ + z) * NC + c, target))
    return pairs


def to_core(array):
    return lax.ppermute(array, "dp", dp_shift(0, 0, 1))


def to_x(array, step):
    return lax.ppermute(array, "mp", [(i, (i + step) % NX) for i in range(NX)])


def columns(array, index, width):
    return lax.dynamic_slice_in_dim(array, index * width, width, axis=1)


def product_kernel(lhs, own, after, opposite, before, *rest):
    out = rest[-1]
    tokens = jnp.concatenate([own[...], after[...], opposite[...], before[...]], axis=0)
    out[0] = jnp.dot(lhs[...], tokens, preferred_element_type=jnp.float32).astype(jnp.bfloat16)


def product(piece, lhs, own, after, opposite, before, carry):
    start, width = PIECES[piece]
    skip = start // BLOCK
    whole = pl.BlockSpec((128, BLOCK), lambda i: (0, skip + i))
    alone = pl.BlockSpec((128, BLOCK), lambda i: (0, i))
    specs = [pl.BlockSpec((256, 512), lambda i: (0, 0)), whole, whole, alone, whole]
    operands = [lhs, own, after, opposite, before]
    aliases = {}
    if carry is not None:
        specs.append(pl.BlockSpec(memory_space=pl.ANY))
        operands.append(carry)
        aliases = {5: 0}
    return pl.pallas_call(
        product_kernel,
        grid=(width // BLOCK,),
        in_specs=specs,
        out_specs=pl.BlockSpec((1, 256, BLOCK), lambda i: (0, 0, skip + i)),
        out_shape=jax.ShapeDtypeStruct((1, 256, D), jnp.bfloat16),
        input_output_aliases=aliases,
        cost_estimate=pl.CostEstimate(flops=2 * 256 * 512 * width, bytes_accessed=1536 * width, transcendentals=0),
        compiler_params=pltpu.CompilerParams(vmem_limit_bytes=24 * 1024 * 1024),
    )(*operands)


def after_that(array, *events):
    return lax.optimization_barrier((array, *events))[0]


def exchange(sends, moves):
    return [lax.ppermute(array, "dp", dp_shift(*move)) for array, move in zip(sends, moves, strict=True)]


def swap_z(array):
    pairs = [(i, i ^ NC) for i in range(NY * NZ * NC)]
    return lax.ppermute(array, "dp", pairs)


VMEM = pl.BlockSpec(memory_space=pltpu.VMEM)
SMEM = pl.BlockSpec(memory_space=pltpu.SMEM)


def local(body, place, operands, shapes):
    return pl.pallas_call(
        body,
        in_specs=[SMEM] + [VMEM] * len(operands),
        out_specs=[VMEM] * len(shapes),
        out_shape=[jax.ShapeDtypeStruct(shape, dtype) for shape, dtype in shapes],
        compiler_params=pltpu.CompilerParams(vmem_limit_bytes=16 * 1024 * 1024),
    )(place, *operands)


def at(block, width):
    return pl.ds(pl.multiple_of(block * width, 128), width)


def half(core):
    return pl.ds(pl.multiple_of(core * 32, 32), 32)


def add_cores(place, grad, theirs, *outs):
    core, y = place[0], place[1]
    for k, out in enumerate(outs):
        piece = at(lax.rem(y + k, NY), 3072)
        out[...] = grad[0, half(core), piece].astype(jnp.float32) + theirs[:, piece].astype(jnp.float32)


def add_y(place, a, b, c, d, kept, sent):
    low = place[4]
    for q in range(4):
        for out, bit in ((kept, low), (sent, 1 - low)):
            piece = at(2 * q + bit, 384)
            out[:, q * 384 : (q + 1) * 384] = (a[:, piece] + b[:, piece]) + (c[:, piece] + d[:, piece])


def add_pair(place, a, b, *outs):
    q = place[3]
    for k, out in enumerate(outs):
        piece = at(lax.rem(q + k, 4), 384)
        out[...] = a[:, piece] + b[:, piece]


def adam(place, a, b, c, d, state, new_state, weights):
    total = (a[...] + b[...]) + (c[...] + d[...])
    new_moment = beta_one * state[1] + (1.0 - beta_one) * total
    new_second = beta_two * state[2] + (1.0 - beta_two) * total * total
    first_hat = new_moment / (1.0 - beta_one**STEP)
    second_hat = new_second / (1.0 - beta_two**STEP)
    new_master = state[0] - learn_rate * (first_hat / (jnp.sqrt(second_hat) + adam_eps) + decay_rate * state[0])
    new_state[0] = new_master
    new_state[1] = new_moment
    new_state[2] = new_second
    weights[...] = new_master.astype(jnp.bfloat16)


def join_ring(place, *refs):
    *parts, out = refs
    width = parts[0].shape[1]
    here = place[3] if width == 384 else place[1]
    for k, part in enumerate(parts):
        out[:, at(lax.rem(here + 4 - k, 4), width)] = part[...]


def join_pair(place, mine, other, out):
    low = place[4]
    for q in range(4):
        piece = slice(q * 384, (q + 1) * 384)
        out[:, at(2 * q + low, 384)] = mine[:, piece]
        out[:, at(2 * q + 1 - low, 384)] = other[:, piece]


def join_cores(place, mine, other, out):
    core = place[0]
    out[half(core), :] = mine[...]
    out[half(1 - core), :] = other[...]


def per_device(grads, master, moment, second, inputs, out_grads):
    index = lax.axis_index("dp")
    x = lax.axis_index("mp")
    core = index % NC
    z = (index // NC) % NZ
    y = index // (NC * NZ)
    first = core == 0
    place = jnp.stack([core, y, z, z // 2, z % 2]).astype(jnp.int32)
    f32, bf16 = jnp.float32, jnp.bfloat16

    before = to_x(inputs, 1)
    after = to_x(inputs, -1)
    lhs = lax.dynamic_slice_in_dim(jnp.concatenate([out_grads, out_grads]), x * 128, 512, axis=0).T

    theirs = to_core(lax.dynamic_slice_in_dim(grads[0], (1 - core) * 32, 32, axis=0))

    state = jnp.stack([master, moment, second])
    kept = lax.dynamic_slice_in_dim(state, core * 32, 32, axis=1)
    got = to_core(after_that(lax.dynamic_slice_in_dim(state, (1 - core) * 32, 32, axis=1), theirs))
    state = jnp.concatenate([jnp.where(first, kept, got), jnp.where(first, got, kept)], axis=2)

    kept, *sent = local(add_cores, place, (grads, theirs), [((32, 3072), f32)] * 4)
    got = exchange(sent, [(k, 0, 0) for k in (1, 2, 3)])
    kept, sent = local(add_y, place, (kept, *got), [((32, 1536), f32)] * 2)
    got = swap_z(sent)
    kept, *sent = local(add_pair, place, (kept, got), [((32, 384), f32)] * 4)
    got = exchange(sent, [(0, 2 * k, 0) for k in (1, 2, 3)])
    state, own = local(adam, place, (kept, *got, state), [((3, 32, 384), f32), ((32, 384), bf16)])

    got = exchange([own] * 3, [(0, 2 * k, 0) for k in (1, 2, 3)])
    (own,) = local(join_ring, place, (own, *got), [((32, 1536), bf16)])
    got = swap_z(own)
    (own,) = local(join_pair, place, (own, got), [((32, 3072), bf16)])
    before, after, own = lax.optimization_barrier((before, after, own))
    opposites = []
    for piece, (start, width) in enumerate(PIECES):
        near, way = ((before, 1), (after, -1))[piece % 2]
        near = near[:, start : start + width]
        if piece >= 2:
            near = after_that(near, opposites[piece - 2])
        opposites.append(to_x(near, way))

    got = exchange([own] * 3, [(k, 0, 0) for k in (1, 2, 3)])
    (own,) = local(join_ring, place, (own, *got), [((32, D), bf16)])

    other = to_core(own)
    (weights,) = local(join_cores, place, (own, other), [((64, D), bf16)])

    left, right = state[:, :, :192], state[:, :, 192:]
    kept = jnp.where(first, left, right)
    got = to_core(after_that(jnp.where(first, right, left), other))
    state = jnp.concatenate([jnp.where(first, kept, got), jnp.where(first, got, kept)], axis=1)

    lhs, weights, state = lax.optimization_barrier((lhs, weights, state))
    carry = None
    for piece in range(4):
        carry = product(piece, lhs, inputs, after, opposites[piece], before, carry)

    return (weights, state[0], state[1], state[2], carry)


def solution(mesh):
    return jax.shard_map(
        per_device,
        mesh=mesh,
        in_specs=(
            P("dp", "mp", None),
            P("mp", "dp"),
            P("mp", "dp"),
            P("mp", "dp"),
            P(("dp", "mp"), None),
            P("dp", "mp"),
        ),
        out_specs=(P("mp", None), P("mp", "dp"), P("mp", "dp"), P("mp", "dp"), P("dp", "mp", None)),
        check_vma=False,
    )
```

```python
import functools

import jax
import jax.numpy as jnp
from jax import lax
from jax.experimental import pallas as pl
from jax.experimental.pallas import tpu as pltpu
from jax.sharding import PartitionSpec as P

STEP = 10

beta_one = 0.9
beta_two = 0.95
learn_rate = 0.05
decay_rate = 0.1
adam_eps = 1e-08

NY, NZ, NC, NX = 4, 8, 2, 4
D = 12288
PIECES = ((0, 5120), (10240, 1024))
VMEM_LIMIT = 20 * 1024 * 1024


def dp_shift(dy, dz, dc):
    pairs = []
    for y in range(NY):
        for z in range(NZ):
            for c in range(NC):
                target = (((y + dy) % NY) * NZ + (z + dz) % NZ) * NC + (c + dc) % NC
                pairs.append(((y * NZ + z) * NC + c, target))
    return pairs


def to_core(array):
    return lax.ppermute(array, "dp", dp_shift(0, 0, 1))


def to_x(array, step):
    return lax.ppermute(array, "mp", [(i, (i + step) % NX) for i in range(NX)])


def columns(array, index, width):
    return lax.dynamic_slice_in_dim(array, index * width, width, axis=1)


def product_kernel(lhs, own, after, before, first, second, *rest):
    out = rest[-1]
    step, half_way = pl.program_id(0), pl.num_programs(0) // 2

    def columns_of(opposite):
        tokens = jnp.concatenate([own[...], after[...], opposite[...], before[...]], axis=0)
        out[0] = jnp.dot(lhs[...], tokens, preferred_element_type=jnp.float32).astype(jnp.bfloat16)

    @pl.when(step < half_way)
    def _():
        columns_of(first)

    @pl.when(step >= half_way)
    def _():
        columns_of(second)


def product(start, block, lhs, own, after, before, first, second, carry, sign_of_next=None):
    steps, skip = first.shape[1] // block, start // block
    whole = pl.BlockSpec((128, block), lambda i: (0, skip + i))
    specs = [
        pl.BlockSpec((256, 512), lambda i: (0, 0)),
        whole,
        whole,
        whole,
        pl.BlockSpec((128, block), lambda i: (0, jnp.minimum(i, steps - 1))),
        pl.BlockSpec((128, block), lambda i: (0, jnp.maximum(i - steps, 0))),
    ]
    operands = [lhs, own, after, before, first, second]
    aliases = {}
    if carry is not None:
        specs.append(pl.BlockSpec(memory_space=pl.ANY))
        operands.append(carry)
        aliases = {6: 0}
    if sign_of_next is not None:
        specs.append(pl.BlockSpec(memory_space=pl.ANY))
        operands.append(sign_of_next)
    width = 2 * first.shape[1]
    return pl.pallas_call(
        product_kernel,
        grid=(2 * steps,),
        in_specs=specs,
        out_specs=pl.BlockSpec((1, 256, block), lambda i: (0, 0, skip + i)),
        out_shape=jax.ShapeDtypeStruct((1, 256, D), jnp.bfloat16),
        input_output_aliases=aliases,
        cost_estimate=pl.CostEstimate(flops=2 * 256 * 512 * width, bytes_accessed=1536 * width, transcendentals=0),
        compiler_params=pltpu.CompilerParams(vmem_limit_bytes=VMEM_LIMIT),
    )(*operands)


def sign(*arrays):
    return jnp.concatenate([array[:16, :128] for array in arrays])


def after_that(array, *events):
    return lax.optimization_barrier((array, *events))[0]


def exchange(sends, moves):
    return [lax.ppermute(array, "dp", dp_shift(*move)) for array, move in zip(sends, moves, strict=True)]


def swap_z(array):
    pairs = [(i, i ^ NC) for i in range(NY * NZ * NC)]
    return lax.ppermute(array, "dp", pairs)


VMEM = pl.BlockSpec(memory_space=pltpu.VMEM)
SMEM = pl.BlockSpec(memory_space=pltpu.SMEM)


def local(body, place, operands, shapes):
    return pl.pallas_call(
        body,
        in_specs=[SMEM] + [VMEM] * len(operands),
        out_specs=[VMEM] * len(shapes),
        out_shape=[jax.ShapeDtypeStruct(shape, dtype) for shape, dtype in shapes],
        cost_estimate=pl.CostEstimate(flops=1024, bytes_accessed=1024, transcendentals=0),
        compiler_params=pltpu.CompilerParams(vmem_limit_bytes=16 * 1024 * 1024),
    )(place, *operands)


def at(block, width):
    return pl.ds(pl.multiple_of(block * width, 128), width)


def half(core):
    return pl.ds(pl.multiple_of(core * 32, 32), 32)


def cut_kernel(places, before, after, *refs):
    outs, sems = refs[:-1], refs[-1]
    copies = []
    for k, (out, start) in enumerate(zip(outs, places)):
        source = (before, after)[k % 2].at[:, start : start + out.shape[1]]
        copies.append(pltpu.make_async_copy(source, out, sems.at[k]))
    for copy in copies:
        copy.start()
    for copy in copies:
        copy.wait()


def cut(pieces, before, after):
    anywhere = pl.BlockSpec(memory_space=pl.ANY)
    places = [start + way * width for start, width in pieces for way in (0, 1)]
    shapes = [jax.ShapeDtypeStruct((128, width), jnp.bfloat16) for _, width in pieces for _ in (0, 1)]
    return pl.pallas_call(
        functools.partial(cut_kernel, places),
        in_specs=[anywhere, anywhere],
        out_specs=[VMEM] * len(shapes),
        out_shape=shapes,
        scratch_shapes=[pltpu.SemaphoreType.DMA((len(shapes),))],
        cost_estimate=pl.CostEstimate(flops=1024, bytes_accessed=1024, transcendentals=0),
        compiler_params=pltpu.CompilerParams(vmem_limit_bytes=16 * 1024 * 1024),
    )(before, after)


def turn(place, out_grads, out):
    for step in range(NX):
        owner = lax.rem(place[5] + step, NX)
        rows = pl.ds(pl.multiple_of(owner * 128, 128), 128)
        out[:, step * 128 : (step + 1) * 128] = out_grads[rows, :].T


def add_cores(place, grad, theirs, *outs):
    core, y = place[0], place[1]
    for k, out in enumerate(outs):
        piece = at(lax.rem(y + k, NY), 3072)
        out[...] = grad[0, half(core), piece].astype(jnp.float32) + theirs[:, piece].astype(jnp.float32)


def add_y(place, a, b, c, d, kept, sent):
    low = place[4]
    for q in range(4):
        for out, bit in ((kept, low), (sent, 1 - low)):
            piece = at(2 * q + bit, 384)
            out[:, q * 384 : (q + 1) * 384] = (a[:, piece] + b[:, piece]) + (c[:, piece] + d[:, piece])


def add_pair(place, a, b, *outs):
    q = place[3]
    for k, out in enumerate(outs):
        piece = at(lax.rem(q + k, 4), 384)
        out[...] = a[:, piece] + b[:, piece]


def adam(place, a, b, c, d, state, new_state, weights):
    total = (a[...] + b[...]) + (c[...] + d[...])
    new_moment = beta_one * state[1] + (1.0 - beta_one) * total
    new_second = beta_two * state[2] + (1.0 - beta_two) * total * total
    first_hat = new_moment / (1.0 - beta_one**STEP)
    second_hat = new_second / (1.0 - beta_two**STEP)
    new_master = state[0] - learn_rate * (first_hat / (jnp.sqrt(second_hat) + adam_eps) + decay_rate * state[0])
    new_state[0] = new_master
    new_state[1] = new_moment
    new_state[2] = new_second
    weights[...] = new_master.astype(jnp.bfloat16)


def join_ring(place, *refs):
    *parts, out = refs
    width = parts[0].shape[1]
    here = place[3] if width == 384 else place[1]
    for k, part in enumerate(parts):
        out[:, at(lax.rem(here + 4 - k, 4), width)] = part[...]


def join_pair(place, mine, other, out):
    low = place[4]
    for q in range(4):
        piece = slice(q * 384, (q + 1) * 384)
        out[:, at(2 * q + low, 384)] = mine[:, piece]
        out[:, at(2 * q + 1 - low, 384)] = other[:, piece]


def join_rows(place, *refs):
    *parts, out = refs
    core, y = place[0], place[1]
    for k in range(NY):
        piece = at(lax.rem(y + NY - k, NY), 3072)
        out[half(core), piece] = parts[k][...]
        out[half(1 - core), piece] = parts[NY + k][...]


def per_device(grads, master, moment, second, inputs, out_grads):
    index = lax.axis_index("dp")
    x = lax.axis_index("mp")
    core = index % NC
    z = (index // NC) % NZ
    y = index // (NC * NZ)
    first = core == 0
    place = jnp.stack([core, y, z, z // 2, z % 2, x]).astype(jnp.int32)
    f32, bf16 = jnp.float32, jnp.bfloat16

    before = to_x(inputs, 1)
    after = to_x(inputs, -1)
    (lhs,) = local(turn, place, (out_grads,), [((256, 512), bf16)])

    theirs = to_core(lax.dynamic_slice_in_dim(grads[0], (1 - core) * 32, 32, axis=0))

    state = jnp.stack([master, moment, second])
    kept = lax.dynamic_slice_in_dim(state, core * 32, 32, axis=1)
    got = to_core(after_that(lax.dynamic_slice_in_dim(state, (1 - core) * 32, 32, axis=1), theirs))
    state = jnp.concatenate([jnp.where(first, kept, got), jnp.where(first, got, kept)], axis=2)

    kept, *sent = local(add_cores, place, (grads, theirs), [((32, 3072), f32)] * 4)
    got = exchange(sent, [(k, 0, 0) for k in (1, 2, 3)])
    kept, sent = local(add_y, place, (kept, *got), [((32, 1536), f32)] * 2)
    got = swap_z(sent)
    kept, *sent = local(add_pair, place, (kept, got), [((32, 384), f32)] * 4)
    got = exchange(sent, [(0, 2 * k, 0) for k in (1, 2, 3)])
    state, own = local(adam, place, (kept, *got, state), [((3, 32, 384), f32), ((32, 384), bf16)])

    got = exchange([own] * 3, [(0, 2 * k, 0) for k in (1, 2, 3)])
    (own,) = local(join_ring, place, (own, *got), [((32, 1536), bf16)])
    got = swap_z(own)

    before, after, own, got = lax.optimization_barrier((before, after, own, got))
    near = cut(PIECES[:1], before, after)
    *near, own, got = lax.optimization_barrier((*near, own, got))
    opposites = [to_x(near[0], 1), to_x(near[1], -1)]

    (own,) = local(join_pair, place, (own, got), [((32, 3072), bf16)])
    got = exchange([own] * 3, [(k, 0, 0) for k in (1, 2, 3)])

    parts = [own, *got]
    others = [to_core(part) for part in parts]
    (weights,) = local(join_rows, place, (*parts, *others), [((64, D), bf16)])

    left, right = state[:, :, :192], state[:, :, 192:]
    kept = jnp.where(first, left, right)
    got = to_core(after_that(jnp.where(first, right, left), others[0]))
    state = jnp.concatenate([jnp.where(first, kept, got), jnp.where(first, got, kept)], axis=1)
    state = [state[0], state[1], state[2]]

    near = cut(PIECES[1:], before, after)
    *near, weights, state[0], state[1], state[2], there = lax.optimization_barrier(
        (*near, weights, *state, sign(*opposites))
    )
    opposites += [to_x(near[0], 1), to_x(near[1], -1)]

    carry = product(PIECES[0][0], 2560, lhs, inputs, after, before, *opposites[:2], None, there)
    carry = product(PIECES[1][0], 1024, lhs, inputs, after, before, *opposites[2:], carry)

    return (weights, state[0], state[1], state[2], carry)


def solution(mesh):
    return jax.shard_map(
        per_device,
        mesh=mesh,
        in_specs=(
            P("dp", "mp", None),
            P("mp", "dp"),
            P("mp", "dp"),
            P("mp", "dp"),
            P(("dp", "mp"), None),
            P("dp", "mp"),
        ),
        out_specs=(P("mp", None), P("mp", "dp"), P("mp", "dp"), P("mp", "dp"), P("dp", "mp", None)),
        check_vma=False,
    )
```

```python
import functools

import jax
import jax.numpy as jnp
from jax import lax
from jax.experimental import pallas as pl
from jax.experimental.pallas import tpu as pltpu
from jax.sharding import PartitionSpec as P

STEP = 10

beta_one = 0.9
beta_two = 0.95
learn_rate = 0.05
decay_rate = 0.1
adam_eps = 1e-08

NY, NZ, NC, NX = 4, 8, 2, 4
D = 12288
PIECES = ((0, 4608), (9216, 1536))
VMEM_LIMIT = 20 * 1024 * 1024


def dp_swap(dy, dz, dc):
    return [(i, i ^ ((dy * NZ + dz) * NC + dc)) for i in range(NY * NZ * NC)]


def to_core(array):
    return lax.ppermute(array, "dp", dp_swap(0, 0, 1))


def swap_x(array, bits):
    return lax.ppermute(array, "mp", [(i, i ^ bits) for i in range(NX)])


def columns(array, index, width):
    return lax.dynamic_slice_in_dim(array, index * width, width, axis=1)


def product_kernel(lhs, own, after, before, first, second, *rest):
    out = rest[-1]
    step, half_way = pl.program_id(0), pl.num_programs(0) // 2

    def columns_of(opposite):
        tokens = jnp.concatenate([own[...], before[...], opposite[...], after[...]], axis=0)
        out[0] = jnp.dot(lhs[...], tokens, preferred_element_type=jnp.float32).astype(jnp.bfloat16)

    @pl.when(step < half_way)
    def _():
        columns_of(first)

    @pl.when(step >= half_way)
    def _():
        columns_of(second)


def product(start, block, lhs, own, after, before, first, second, carry, sign_of_next=None):
    steps, skip = first.shape[1] // block, start // block
    whole = pl.BlockSpec((128, block), lambda i: (0, skip + i))
    specs = [
        pl.BlockSpec((256, 512), lambda i: (0, 0)),
        whole,
        whole,
        whole,
        pl.BlockSpec((128, block), lambda i: (0, jnp.minimum(i, steps - 1))),
        pl.BlockSpec((128, block), lambda i: (0, jnp.maximum(i - steps, 0))),
    ]
    operands = [lhs, own, after, before, first, second]
    aliases = {}
    if carry is not None:
        specs.append(pl.BlockSpec(memory_space=pl.ANY))
        operands.append(carry)
        aliases = {6: 0}
    if sign_of_next is not None:
        specs.append(pl.BlockSpec(memory_space=pl.ANY))
        operands.append(sign_of_next)
    width = 2 * first.shape[1]
    return pl.pallas_call(
        product_kernel,
        grid=(2 * steps,),
        in_specs=specs,
        out_specs=pl.BlockSpec((1, 256, block), lambda i: (0, 0, skip + i)),
        out_shape=jax.ShapeDtypeStruct((1, 256, D), jnp.bfloat16),
        input_output_aliases=aliases,
        cost_estimate=pl.CostEstimate(flops=2 * 256 * 512 * width, bytes_accessed=1536 * width, transcendentals=0),
        compiler_params=pltpu.CompilerParams(vmem_limit_bytes=VMEM_LIMIT),
    )(*operands)


def sign(*arrays):
    return jnp.concatenate([array[:16, :128] for array in arrays])


def after_that(array, *events):
    return lax.optimization_barrier((array, *events))[0]


def exchange(sends, moves):
    return [lax.ppermute(array, "dp", dp_swap(*move)) for array, move in zip(sends, moves, strict=True)]


def swap_z(array):
    return lax.ppermute(array, "dp", dp_swap(0, 1, 0))


VMEM = pl.BlockSpec(memory_space=pltpu.VMEM)
SMEM = pl.BlockSpec(memory_space=pltpu.SMEM)


def local(body, place, operands, shapes):
    return pl.pallas_call(
        body,
        in_specs=[SMEM] + [VMEM] * len(operands),
        out_specs=[VMEM] * len(shapes),
        out_shape=[jax.ShapeDtypeStruct(shape, dtype) for shape, dtype in shapes],
        cost_estimate=pl.CostEstimate(flops=1024, bytes_accessed=1024, transcendentals=0),
        compiler_params=pltpu.CompilerParams(vmem_limit_bytes=16 * 1024 * 1024),
    )(place, *operands)


def at(block, width):
    return pl.ds(pl.multiple_of(block * width, 128), width)


def half(core):
    return pl.ds(pl.multiple_of(core * 32, 32), 32)


def cut_kernel(places, before, after, *refs):
    outs, sems = refs[:-1], refs[-1]
    copies = []
    for k, (out, start) in enumerate(zip(outs, places)):
        source = (before, after)[k % 2].at[:, start : start + out.shape[1]]
        copies.append(pltpu.make_async_copy(source, out, sems.at[k]))
    for copy in copies:
        copy.start()
    for copy in copies:
        copy.wait()


def cut(pieces, before, after):
    anywhere = pl.BlockSpec(memory_space=pl.ANY)
    places = [start + way * width for start, width in pieces for way in (0, 1)]
    shapes = [jax.ShapeDtypeStruct((128, width), jnp.bfloat16) for _, width in pieces for _ in (0, 1)]
    return pl.pallas_call(
        functools.partial(cut_kernel, places),
        in_specs=[anywhere, anywhere],
        out_specs=[VMEM] * len(shapes),
        out_shape=shapes,
        scratch_shapes=[pltpu.SemaphoreType.DMA((len(shapes),))],
        cost_estimate=pl.CostEstimate(flops=1024, bytes_accessed=1024, transcendentals=0),
        compiler_params=pltpu.CompilerParams(vmem_limit_bytes=16 * 1024 * 1024),
    )(before, after)


def turn(place, out_grads, out):
    for step in range(NX):
        owner = place[5] ^ step
        rows = pl.ds(pl.multiple_of(owner * 128, 128), 128)
        out[:, step * 128 : (step + 1) * 128] = out_grads[rows, :].T


def halves_kernel(place, grads, mine, sent, sems):
    core = place[0]
    copies = [
        pltpu.make_async_copy(grads.at[0, half(1 - core), :], sent, sems.at[0]),
        pltpu.make_async_copy(grads.at[0, half(core), :], mine, sems.at[1]),
    ]
    for copy in copies:
        copy.start()
    for copy in copies:
        copy.wait()


def halves(place, grads):
    shape = jax.ShapeDtypeStruct((32, D), jnp.bfloat16)
    return pl.pallas_call(
        halves_kernel,
        in_specs=[SMEM, pl.BlockSpec(memory_space=pltpu.HBM)],
        out_specs=[VMEM, VMEM],
        out_shape=[shape, shape],
        scratch_shapes=[pltpu.SemaphoreType.DMA((2,))],
        cost_estimate=pl.CostEstimate(flops=1024, bytes_accessed=1024, transcendentals=0),
        compiler_params=pltpu.CompilerParams(vmem_limit_bytes=8 * 1024 * 1024),
    )(place, grads)


def add_cores(place, mine, theirs, *outs):
    for k, out in enumerate(outs):
        piece = at(place[1] ^ k, 3072)
        out[...] = mine[:, piece].astype(jnp.float32) + theirs[:, piece].astype(jnp.float32)


def add_y(place, a, b, c, d, kept, sent):
    low = place[4]
    for q in range(4):
        for out, bit in ((kept, low), (sent, 1 - low)):
            piece = at(2 * q + bit, 384)
            out[:, q * 384 : (q + 1) * 384] = (a[:, piece] + b[:, piece]) + (c[:, piece] + d[:, piece])


def add_pair(place, a, b, *outs):
    q = place[3]
    for k, out in enumerate(outs):
        piece = at(q ^ k, 384)
        out[...] = a[:, piece] + b[:, piece]


def adam(place, a, b, c, d, state, new_state, weights):
    total = (a[...] + b[...]) + (c[...] + d[...])
    new_moment = beta_one * state[1] + (1.0 - beta_one) * total
    new_second = beta_two * state[2] + (1.0 - beta_two) * total * total
    first_hat = new_moment / (1.0 - beta_one**STEP)
    second_hat = new_second / (1.0 - beta_two**STEP)
    new_master = state[0] - learn_rate * (first_hat / (jnp.sqrt(second_hat) + adam_eps) + decay_rate * state[0])
    new_state[0] = new_master
    new_state[1] = new_moment
    new_state[2] = new_second
    weights[...] = new_master.astype(jnp.bfloat16)


def join_ring(place, *refs):
    *parts, out = refs
    width = parts[0].shape[1]
    here = place[3] if width == 384 else place[1]
    for k, part in enumerate(parts):
        out[:, at(here ^ k, width)] = part[...]


def join_pair(place, mine, other, out):
    low = place[4]
    for q in range(4):
        piece = slice(q * 384, (q + 1) * 384)
        out[:, at(2 * q + low, 384)] = mine[:, piece]
        out[:, at(2 * q + 1 - low, 384)] = other[:, piece]


def join_rows(place, *refs):
    *parts, out = refs
    core, y = place[0], place[1]
    for k in range(NY):
        piece = at(y ^ k, 3072)
        out[half(core), piece] = parts[k][...]
        out[half(1 - core), piece] = parts[NY + k][...]


def per_device(grads, master, moment, second, inputs, out_grads):
    index = lax.axis_index("dp")
    x = lax.axis_index("mp")
    core = index % NC
    z = (index // NC) % NZ
    y = index // (NC * NZ)
    first = core == 0
    place = jnp.stack([core, y, z, z // 2, z % 2, x]).astype(jnp.int32)
    f32, bf16 = jnp.float32, jnp.bfloat16

    before = swap_x(inputs, 1)
    after = swap_x(inputs, 3)
    (lhs,) = local(turn, place, (out_grads,), [((256, 512), bf16)])

    mine, sent = halves(place, grads)
    theirs = to_core(sent)

    state = jnp.stack([master, moment, second])
    kept = lax.dynamic_slice_in_dim(state, core * 32, 32, axis=1)
    got = to_core(after_that(lax.dynamic_slice_in_dim(state, (1 - core) * 32, 32, axis=1), theirs))
    state = jnp.concatenate([jnp.where(first, kept, got), jnp.where(first, got, kept)], axis=2)

    kept, *sent = local(add_cores, place, (mine, theirs), [((32, 3072), f32)] * 4)
    got = exchange(sent, [(k, 0, 0) for k in (1, 2, 3)])
    kept, sent = local(add_y, place, (kept, *got), [((32, 1536), f32)] * 2)
    got = swap_z(sent)
    kept, *sent = local(add_pair, place, (kept, got), [((32, 384), f32)] * 4)
    got = exchange(sent, [(0, 2 * k, 0) for k in (1, 2, 3)])
    state, own = local(adam, place, (kept, *got, state), [((3, 32, 384), f32), ((32, 384), bf16)])

    got = exchange([own] * 3, [(0, 2 * k, 0) for k in (1, 2, 3)])
    (own,) = local(join_ring, place, (own, *got), [((32, 1536), bf16)])

    before, after, own = lax.optimization_barrier((before, after, own))
    near = cut(PIECES[:1], before, after)
    *near, own = lax.optimization_barrier((*near, own))
    opposites = [swap_x(near[0], 3), swap_x(near[1], 1)]

    got = swap_z(own)
    (own,) = local(join_pair, place, (own, got), [((32, 3072), bf16)])
    got = exchange([own] * 3, [(k, 0, 0) for k in (1, 2, 3)])

    near = cut(PIECES[1:], before, after)
    *near, got0, got1, got2 = lax.optimization_barrier((*near, *got))
    opposites += [swap_x(near[0], 3), swap_x(near[1], 1)]
    parts = [own, got0, got1, got2]
    others = [to_core(part) for part in parts]
    (weights,) = local(join_rows, place, (*parts, *others), [((64, D), bf16)])

    left, right = state[:, :, :192], state[:, :, 192:]
    kept = jnp.where(first, left, right)
    got = to_core(after_that(jnp.where(first, right, left), others[0]))
    state = jnp.concatenate([jnp.where(first, kept, got), jnp.where(first, got, kept)], axis=1)
    state = [state[0], state[1], state[2]]

    weights, state[0], state[1], state[2], lhs = lax.optimization_barrier((weights, *state, lhs))
    carry = product(PIECES[0][0], 2304, lhs, inputs, after, before, *opposites[:2], None)
    carry = product(PIECES[1][0], 1536, lhs, inputs, after, before, *opposites[2:], carry)

    return (weights, state[0], state[1], state[2], carry)


def solution(mesh):
    return jax.shard_map(
        per_device,
        mesh=mesh,
        in_specs=(
            P("dp", "mp", None),
            P("mp", "dp"),
            P("mp", "dp"),
            P("mp", "dp"),
            P(("dp", "mp"), None),
            P("dp", "mp"),
        ),
        out_specs=(P("mp", None), P("mp", "dp"), P("mp", "dp"), P("mp", "dp"), P("dp", "mp", None)),
        check_vma=False,
    )
```

```python
import functools

import jax
import jax.numpy as jnp
from jax import lax
from jax.experimental import pallas as pl
from jax.experimental.pallas import tpu as pltpu
from jax.sharding import PartitionSpec as P

STEP = 10

beta_one = 0.9
beta_two = 0.95
learn_rate = 0.05
decay_rate = 0.1
adam_eps = 1e-08

NY, NZ, NC, NX = 4, 8, 2, 4
D = 12288
PIECES = ((0, 4608), (9216, 1536))
VMEM_LIMIT = 20 * 1024 * 1024


def dp_swap(dy, dz, dc):
    return [(i, i ^ ((dy * NZ + dz) * NC + dc)) for i in range(NY * NZ * NC)]


def to_core(array):
    return lax.ppermute(array, "dp", dp_swap(0, 0, 1))


def swap_x(array, bits):
    return lax.ppermute(array, "mp", [(i, i ^ bits) for i in range(NX)])


def columns(array, index, width):
    return lax.dynamic_slice_in_dim(array, index * width, width, axis=1)


def product_kernel(lhs, own, after, before, first, second, *rest):
    out = rest[-1]
    step, half_way = pl.program_id(0), pl.num_programs(0) // 2

    def columns_of(opposite):
        tokens = jnp.concatenate([own[...], before[...], after[...], opposite[...]], axis=0)
        out[0] = jnp.dot(lhs[...], tokens, preferred_element_type=jnp.float32).astype(jnp.bfloat16)

    @pl.when(step < half_way)
    def _():
        columns_of(first)

    @pl.when(step >= half_way)
    def _():
        columns_of(second)


def product(start, block, lhs, own, after, before, first, second, carry, sign_of_next=None):
    steps, skip = first.shape[1] // block, start // block
    whole = pl.BlockSpec((128, block), lambda i: (0, skip + i))
    specs = [
        pl.BlockSpec((256, 512), lambda i: (0, 0)),
        whole,
        whole,
        whole,
        pl.BlockSpec((128, block), lambda i: (0, jnp.minimum(i, steps - 1))),
        pl.BlockSpec((128, block), lambda i: (0, jnp.maximum(i - steps, 0))),
    ]
    operands = [lhs, own, after, before, first, second]
    aliases = {}
    if carry is not None:
        specs.append(pl.BlockSpec(memory_space=pl.ANY))
        operands.append(carry)
        aliases = {6: 0}
    if sign_of_next is not None:
        specs.append(pl.BlockSpec(memory_space=pl.ANY))
        operands.append(sign_of_next)
    width = 2 * first.shape[1]
    return pl.pallas_call(
        product_kernel,
        grid=(2 * steps,),
        in_specs=specs,
        out_specs=pl.BlockSpec((1, 256, block), lambda i: (0, 0, skip + i)),
        out_shape=jax.ShapeDtypeStruct((1, 256, D), jnp.bfloat16),
        input_output_aliases=aliases,
        cost_estimate=pl.CostEstimate(flops=2 * 256 * 512 * width, bytes_accessed=1536 * width, transcendentals=0),
        compiler_params=pltpu.CompilerParams(vmem_limit_bytes=VMEM_LIMIT),
    )(*operands)


def near_kernel(lhs, own, after, before, out, done):
    tokens = jnp.concatenate([own[...], before[...], after[...]], axis=0)
    out[...] = jnp.dot(lhs[:, :384], tokens, preferred_element_type=jnp.float32)
    done[...] = jnp.zeros_like(done)


def near_product(piece, lhs, own, after, before):
    start, width = piece
    whole = pl.BlockSpec((128, width), lambda i: (0, start // width + i))
    return pl.pallas_call(
        near_kernel,
        grid=(2,),
        in_specs=[pl.BlockSpec((256, 512), lambda i: (0, 0)), whole, whole, whole],
        out_specs=[pl.BlockSpec((256, width), lambda i: (0, i)), pl.BlockSpec((8, 128), lambda i: (0, 0))],
        out_shape=[jax.ShapeDtypeStruct((256, 2 * width), jnp.float32), jax.ShapeDtypeStruct((8, 128), jnp.float32)],
        compiler_params=pltpu.CompilerParams(vmem_limit_bytes=VMEM_LIMIT),
    )(lhs, own, after, before)


def far_kernel(lhs, summed, first, second, carry, out):
    step = pl.program_id(0)

    def columns_of(opposite):
        far = jnp.dot(lhs[:, 384:], opposite[...], preferred_element_type=jnp.float32)
        out[0] = (summed[...] + far).astype(jnp.bfloat16)

    @pl.when(step == 0)
    def _():
        columns_of(first)

    @pl.when(step == 1)
    def _():
        columns_of(second)


def far_product(piece, lhs, summed, first, second, carry):
    start, width = piece
    alone = pl.BlockSpec((128, width), lambda i: (0, 0))
    return pl.pallas_call(
        far_kernel,
        grid=(2,),
        in_specs=[
            pl.BlockSpec((256, 512), lambda i: (0, 0)),
            pl.BlockSpec((256, width), lambda i: (0, i)),
            alone,
            alone,
            pl.BlockSpec(memory_space=pl.ANY),
        ],
        out_specs=pl.BlockSpec((1, 256, width), lambda i: (0, 0, start // width + i)),
        out_shape=jax.ShapeDtypeStruct((1, 256, D), jnp.bfloat16),
        input_output_aliases={4: 0},
        cost_estimate=pl.CostEstimate(flops=512 * 256 * width, bytes_accessed=2048 * width, transcendentals=0),
        compiler_params=pltpu.CompilerParams(vmem_limit_bytes=VMEM_LIMIT),
    )(lhs, summed, first, second, carry)


def sign(*arrays):
    return jnp.concatenate([array[:16, :128] for array in arrays])


def after_that(array, *events):
    return lax.optimization_barrier((array, *events))[0]


def exchange(sends, moves):
    return [lax.ppermute(array, "dp", dp_swap(*move)) for array, move in zip(sends, moves, strict=True)]


def swap_z(array):
    return lax.ppermute(array, "dp", dp_swap(0, 1, 0))


VMEM = pl.BlockSpec(memory_space=pltpu.VMEM)
SMEM = pl.BlockSpec(memory_space=pltpu.SMEM)


def local(body, place, operands, shapes):
    return pl.pallas_call(
        body,
        in_specs=[SMEM] + [VMEM] * len(operands),
        out_specs=[VMEM] * len(shapes),
        out_shape=[jax.ShapeDtypeStruct(shape, dtype) for shape, dtype in shapes],
        cost_estimate=pl.CostEstimate(flops=1024, bytes_accessed=1024, transcendentals=0),
        compiler_params=pltpu.CompilerParams(vmem_limit_bytes=16 * 1024 * 1024),
    )(place, *operands)


def at(block, width):
    return pl.ds(pl.multiple_of(block * width, 128), width)


def half(core):
    return pl.ds(pl.multiple_of(core * 32, 32), 32)


def cut_kernel(places, before, after, *refs):
    outs, sems = refs[:-1], refs[-1]
    copies = []
    for k, (out, start) in enumerate(zip(outs, places)):
        source = (before, after)[k % 2].at[:, start : start + out.shape[1]]
        copies.append(pltpu.make_async_copy(source, out, sems.at[k]))
    for copy in copies:
        copy.start()
    for copy in copies:
        copy.wait()


def cut(pieces, before, after):
    anywhere = pl.BlockSpec(memory_space=pl.ANY)
    places = [start + way * width for start, width in pieces for way in (0, 1)]
    shapes = [jax.ShapeDtypeStruct((128, width), jnp.bfloat16) for _, width in pieces for _ in (0, 1)]
    return pl.pallas_call(
        functools.partial(cut_kernel, places),
        in_specs=[anywhere, anywhere],
        out_specs=[VMEM] * len(shapes),
        out_shape=shapes,
        scratch_shapes=[pltpu.SemaphoreType.DMA((len(shapes),))],
        cost_estimate=pl.CostEstimate(flops=1024, bytes_accessed=1024, transcendentals=0),
        compiler_params=pltpu.CompilerParams(vmem_limit_bytes=16 * 1024 * 1024),
    )(before, after)


def turn(place, out_grads, out):
    for step in range(NX):
        owner = place[5] ^ (0, 1, 3, 2)[step]
        rows = pl.ds(pl.multiple_of(owner * 128, 128), 128)
        out[:, step * 128 : (step + 1) * 128] = out_grads[rows, :].T


def halves_kernel(place, grads, mine, sent, sems):
    core = place[0]
    copies = [
        pltpu.make_async_copy(grads.at[0, half(1 - core), :], sent, sems.at[0]),
        pltpu.make_async_copy(grads.at[0, half(core), :], mine, sems.at[1]),
    ]
    for copy in copies:
        copy.start()
    for copy in copies:
        copy.wait()


def halves(place, grads):
    shape = jax.ShapeDtypeStruct((32, D), jnp.bfloat16)
    return pl.pallas_call(
        halves_kernel,
        in_specs=[SMEM, pl.BlockSpec(memory_space=pltpu.HBM)],
        out_specs=[VMEM, VMEM],
        out_shape=[shape, shape],
        scratch_shapes=[pltpu.SemaphoreType.DMA((2,))],
        cost_estimate=pl.CostEstimate(flops=1024, bytes_accessed=1024, transcendentals=0),
        compiler_params=pltpu.CompilerParams(vmem_limit_bytes=8 * 1024 * 1024),
    )(place, grads)


def add_cores(place, mine, theirs, *outs):
    for k, out in enumerate(outs):
        piece = at(place[1] ^ k, 3072)
        out[...] = mine[:, piece].astype(jnp.float32) + theirs[:, piece].astype(jnp.float32)


def add_y(place, a, b, c, d, kept, sent):
    low = place[4]
    for q in range(4):
        for out, bit in ((kept, low), (sent, 1 - low)):
            piece = at(2 * q + bit, 384)
            out[:, q * 384 : (q + 1) * 384] = (a[:, piece] + b[:, piece]) + (c[:, piece] + d[:, piece])


def add_pair(place, a, b, *outs):
    q = place[3]
    for k, out in enumerate(outs):
        piece = at(q ^ k, 384)
        out[...] = a[:, piece] + b[:, piece]


def adam(place, a, b, c, d, state, new_state, weights):
    total = (a[...] + b[...]) + (c[...] + d[...])
    new_moment = beta_one * state[1] + (1.0 - beta_one) * total
    new_second = beta_two * state[2] + (1.0 - beta_two) * total * total
    first_hat = new_moment / (1.0 - beta_one**STEP)
    second_hat = new_second / (1.0 - beta_two**STEP)
    new_master = state[0] - learn_rate * (first_hat / (jnp.sqrt(second_hat) + adam_eps) + decay_rate * state[0])
    new_state[0] = new_master
    new_state[1] = new_moment
    new_state[2] = new_second
    weights[...] = new_master.astype(jnp.bfloat16)


def join_ring(place, *refs):
    *parts, out = refs
    width = parts[0].shape[1]
    here = place[3] if width == 384 else place[1]
    for k, part in enumerate(parts):
        out[:, at(here ^ k, width)] = part[...]


def join_pair(place, mine, other, out):
    low = place[4]
    for q in range(4):
        piece = slice(q * 384, (q + 1) * 384)
        out[:, at(2 * q + low, 384)] = mine[:, piece]
        out[:, at(2 * q + 1 - low, 384)] = other[:, piece]


def join_rows(place, *refs):
    *parts, out = refs
    core, y = place[0], place[1]
    for k in range(NY):
        piece = at(y ^ k, 3072)
        out[half(core), piece] = parts[k][...]
        out[half(1 - core), piece] = parts[NY + k][...]


def per_device(grads, master, moment, second, inputs, out_grads):
    index = lax.axis_index("dp")
    x = lax.axis_index("mp")
    core = index % NC
    z = (index // NC) % NZ
    y = index // (NC * NZ)
    first = core == 0
    place = jnp.stack([core, y, z, z // 2, z % 2, x]).astype(jnp.int32)
    f32, bf16 = jnp.float32, jnp.bfloat16

    before = swap_x(inputs, 1)
    after = swap_x(inputs, 3)
    (lhs,) = local(turn, place, (out_grads,), [((256, 512), bf16)])

    mine, sent = halves(place, grads)
    theirs = to_core(sent)

    state = jnp.stack([master, moment, second])
    kept = lax.dynamic_slice_in_dim(state, core * 32, 32, axis=1)
    got = to_core(after_that(lax.dynamic_slice_in_dim(state, (1 - core) * 32, 32, axis=1), theirs))
    state = jnp.concatenate([jnp.where(first, kept, got), jnp.where(first, got, kept)], axis=2)

    kept, *sent = local(add_cores, place, (mine, theirs), [((32, 3072), f32)] * 4)
    got = exchange(sent, [(k, 0, 0) for k in (1, 2, 3)])
    kept, sent = local(add_y, place, (kept, *got), [((32, 1536), f32)] * 2)
    got = swap_z(sent)
    kept, *sent = local(add_pair, place, (kept, got), [((32, 384), f32)] * 4)
    got = exchange(sent, [(0, 2 * k, 0) for k in (1, 2, 3)])
    state, own = local(adam, place, (kept, *got, state), [((3, 32, 384), f32), ((32, 384), bf16)])

    got = exchange([own] * 3, [(0, 2 * k, 0) for k in (1, 2, 3)])
    (own,) = local(join_ring, place, (own, *got), [((32, 1536), bf16)])

    before, after, own = lax.optimization_barrier((before, after, own))
    near = cut(PIECES[:1], before, after)
    *near, own = lax.optimization_barrier((*near, own))
    opposites = [swap_x(near[0], 3), swap_x(near[1], 1)]

    got = swap_z(own)
    (own,) = local(join_pair, place, (own, got), [((32, 3072), bf16)])
    got = exchange([own] * 3, [(k, 0, 0) for k in (1, 2, 3)])

    near = cut(PIECES[1:], before, after)
    summed, there = near_product(PIECES[1], lhs, inputs, after, before)
    *near, got0, got1, got2, there = lax.optimization_barrier((*near, *got, there))
    opposites += [swap_x(near[0], 3), swap_x(near[1], 1)]
    parts = [own, got0, got1, got2]
    others = [to_core(part) for part in parts]
    (weights,) = local(join_rows, place, (*parts, *others), [((64, D), bf16)])

    left, right = state[:, :, :192], state[:, :, 192:]
    kept = jnp.where(first, left, right)
    got = to_core(after_that(jnp.where(first, right, left), others[0]))
    state = jnp.concatenate([jnp.where(first, kept, got), jnp.where(first, got, kept)], axis=1)
    state = [state[0], state[1], state[2]]

    weights, state[0], state[1], state[2], there = lax.optimization_barrier((weights, *state, there))
    carry = product(PIECES[0][0], 2304, lhs, inputs, after, before, *opposites[:2], None, there)
    carry = far_product(PIECES[1], lhs, summed, *opposites[2:], carry)

    return (weights, state[0], state[1], state[2], carry)


def solution(mesh):
    return jax.shard_map(
        per_device,
        mesh=mesh,
        in_specs=(
            P("dp", "mp", None),
            P("mp", "dp"),
            P("mp", "dp"),
            P("mp", "dp"),
            P(("dp", "mp"), None),
            P("dp", "mp"),
        ),
        out_specs=(P("mp", None), P("mp", "dp"), P("mp", "dp"), P("mp", "dp"), P("dp", "mp", None)),
        check_vma=False,
    )
```

```python
import functools

import jax
import jax.numpy as jnp
from jax import lax
from jax.experimental import pallas as pl
from jax.experimental.pallas import tpu as pltpu
from jax.sharding import PartitionSpec as P

STEP = 10

beta_one = 0.9
beta_two = 0.95
learn_rate = 0.05
decay_rate = 0.1
adam_eps = 1e-08

NY, NZ, NC, NX = 4, 8, 2, 4
D = 12288
PIECES = ((0, 4608), (9216, 1536))
VMEM_LIMIT = 20 * 1024 * 1024


def dp_swap(dy, dz, dc):
    return [(i, i ^ ((dy * NZ + dz) * NC + dc)) for i in range(NY * NZ * NC)]


def to_core(array):
    return lax.ppermute(array, "dp", dp_swap(0, 0, 1))


def swap_x(array, bits):
    return lax.ppermute(array, "mp", [(i, i ^ bits) for i in range(NX)])


def columns(array, index, width):
    return lax.dynamic_slice_in_dim(array, index * width, width, axis=1)


def product_kernel(lhs, own, after, before, first, second, *rest):
    out = rest[-1]
    step, half_way = pl.program_id(0), pl.num_programs(0) // 2

    def columns_of(opposite):
        tokens = jnp.concatenate([own[...], before[...], after[...], opposite[...]], axis=0)
        out[0] = jnp.dot(lhs[...], tokens, preferred_element_type=jnp.float32).astype(jnp.bfloat16)

    @pl.when(step < half_way)
    def _():
        columns_of(first)

    @pl.when(step >= half_way)
    def _():
        columns_of(second)


def product(start, block, lhs, own, after, before, first, second, carry, sign_of_next=None):
    steps, skip = first.shape[1] // block, start // block
    whole = pl.BlockSpec((128, block), lambda i: (0, skip + i))
    specs = [
        pl.BlockSpec((256, 512), lambda i: (0, 0)),
        whole,
        whole,
        whole,
        pl.BlockSpec((128, block), lambda i: (0, jnp.minimum(i, steps - 1))),
        pl.BlockSpec((128, block), lambda i: (0, jnp.maximum(i - steps, 0))),
    ]
    operands = [lhs, own, after, before, first, second]
    aliases = {}
    if carry is not None:
        specs.append(pl.BlockSpec(memory_space=pl.ANY))
        operands.append(carry)
        aliases = {6: 0}
    if sign_of_next is not None:
        specs.append(pl.BlockSpec(memory_space=pl.ANY))
        operands.append(sign_of_next)
    width = 2 * first.shape[1]
    return pl.pallas_call(
        product_kernel,
        grid=(2 * steps,),
        in_specs=specs,
        out_specs=pl.BlockSpec((1, 256, block), lambda i: (0, 0, skip + i)),
        out_shape=jax.ShapeDtypeStruct((1, 256, D), jnp.bfloat16),
        input_output_aliases=aliases,
        cost_estimate=pl.CostEstimate(flops=2 * 256 * 512 * width, bytes_accessed=1536 * width, transcendentals=0),
        compiler_params=pltpu.CompilerParams(vmem_limit_bytes=32 * 1024 * 1024),
    )(*operands)


def near_kernel(lhs, own, after, before, out, done):
    tokens = jnp.concatenate([own[...], before[...], after[...]], axis=0)
    out[...] = jnp.dot(lhs[:, :384], tokens, preferred_element_type=jnp.float32)
    done[...] = jnp.zeros_like(done)


def near_product(piece, lhs, own, after, before):
    start, width = piece
    whole = pl.BlockSpec((128, width), lambda i: (0, start // width + i))
    return pl.pallas_call(
        near_kernel,
        grid=(2,),
        in_specs=[pl.BlockSpec((256, 512), lambda i: (0, 0)), whole, whole, whole],
        out_specs=[pl.BlockSpec((256, width), lambda i: (0, i)), pl.BlockSpec((8, 128), lambda i: (0, 0))],
        out_shape=[jax.ShapeDtypeStruct((256, 2 * width), jnp.float32), jax.ShapeDtypeStruct((8, 128), jnp.float32)],
        compiler_params=pltpu.CompilerParams(vmem_limit_bytes=VMEM_LIMIT),
    )(lhs, own, after, before)


def far_kernel(lhs, summed, first, second, carry, out):
    step = pl.program_id(0)

    def columns_of(opposite):
        far = jnp.dot(lhs[:, 384:], opposite[...], preferred_element_type=jnp.float32)
        out[0] = (summed[...] + far).astype(jnp.bfloat16)

    @pl.when(step == 0)
    def _():
        columns_of(first)

    @pl.when(step == 1)
    def _():
        columns_of(second)


def far_product(piece, lhs, summed, first, second, carry):
    start, width = piece
    alone = pl.BlockSpec((128, width), lambda i: (0, 0))
    return pl.pallas_call(
        far_kernel,
        grid=(2,),
        in_specs=[
            pl.BlockSpec((256, 512), lambda i: (0, 0)),
            pl.BlockSpec((256, width), lambda i: (0, i)),
            alone,
            alone,
            pl.BlockSpec(memory_space=pl.ANY),
        ],
        out_specs=pl.BlockSpec((1, 256, width), lambda i: (0, 0, start // width + i)),
        out_shape=jax.ShapeDtypeStruct((1, 256, D), jnp.bfloat16),
        input_output_aliases={4: 0},
        cost_estimate=pl.CostEstimate(flops=512 * 256 * width, bytes_accessed=2048 * width, transcendentals=0),
        compiler_params=pltpu.CompilerParams(vmem_limit_bytes=VMEM_LIMIT),
    )(lhs, summed, first, second, carry)


def sign(*arrays):
    return jnp.concatenate([array[:16, :128] for array in arrays])


def after_that(array, *events):
    return lax.optimization_barrier((array, *events))[0]


def exchange(sends, moves):
    return [lax.ppermute(array, "dp", dp_swap(*move)) for array, move in zip(sends, moves, strict=True)]


def swap_z(array):
    return lax.ppermute(array, "dp", dp_swap(0, 1, 0))


VMEM = pl.BlockSpec(memory_space=pltpu.VMEM)
SMEM = pl.BlockSpec(memory_space=pltpu.SMEM)


def local(body, place, operands, shapes):
    return pl.pallas_call(
        body,
        in_specs=[SMEM] + [VMEM] * len(operands),
        out_specs=[VMEM] * len(shapes),
        out_shape=[jax.ShapeDtypeStruct(shape, dtype) for shape, dtype in shapes],
        cost_estimate=pl.CostEstimate(flops=1024, bytes_accessed=1024, transcendentals=0),
        compiler_params=pltpu.CompilerParams(vmem_limit_bytes=16 * 1024 * 1024),
    )(place, *operands)


def at(block, width):
    return pl.ds(pl.multiple_of(block * width, 128), width)


def half(core):
    return pl.ds(pl.multiple_of(core * 32, 32), 32)


def cut_kernel(places, before, after, *refs):
    outs, sems = refs[:-1], refs[-1]
    copies = []
    for k, (out, start) in enumerate(zip(outs, places)):
        source = (before, after)[k % 2].at[:, start : start + out.shape[1]]
        copies.append(pltpu.make_async_copy(source, out, sems.at[k]))
    for copy in copies:
        copy.start()
    for copy in copies:
        copy.wait()


def cut(pieces, before, after):
    anywhere = pl.BlockSpec(memory_space=pl.ANY)
    places = [start + way * width for start, width in pieces for way in (0, 1)]
    shapes = [jax.ShapeDtypeStruct((128, width), jnp.bfloat16) for _, width in pieces for _ in (0, 1)]
    return pl.pallas_call(
        functools.partial(cut_kernel, places),
        in_specs=[anywhere, anywhere],
        out_specs=[VMEM] * len(shapes),
        out_shape=shapes,
        scratch_shapes=[pltpu.SemaphoreType.DMA((len(shapes),))],
        cost_estimate=pl.CostEstimate(flops=1024, bytes_accessed=1024, transcendentals=0),
        compiler_params=pltpu.CompilerParams(vmem_limit_bytes=16 * 1024 * 1024),
    )(before, after)


def turn(place, out_grads, out):
    for step in range(NX):
        owner = place[5] ^ (0, 1, 3, 2)[step]
        rows = pl.ds(pl.multiple_of(owner * 128, 128), 128)
        out[:, step * 128 : (step + 1) * 128] = out_grads[rows, :].T


def halves_kernel(place, grads, mine, sent, sems):
    core = place[0]
    copies = [
        pltpu.make_async_copy(grads.at[0, half(1 - core), :], sent, sems.at[0]),
        pltpu.make_async_copy(grads.at[0, half(core), :], mine, sems.at[1]),
    ]
    for copy in copies:
        copy.start()
    for copy in copies:
        copy.wait()


def halves(place, grads):
    shape = jax.ShapeDtypeStruct((32, D), jnp.bfloat16)
    return pl.pallas_call(
        halves_kernel,
        in_specs=[SMEM, pl.BlockSpec(memory_space=pltpu.HBM)],
        out_specs=[VMEM, VMEM],
        out_shape=[shape, shape],
        scratch_shapes=[pltpu.SemaphoreType.DMA((2,))],
        cost_estimate=pl.CostEstimate(flops=1024, bytes_accessed=1024, transcendentals=0),
        compiler_params=pltpu.CompilerParams(vmem_limit_bytes=8 * 1024 * 1024),
    )(place, grads)


def add_cores(place, mine, theirs, *outs):
    for k, out in enumerate(outs):
        piece = at(place[1] ^ k, 3072)
        out[...] = mine[:, piece].astype(jnp.float32) + theirs[:, piece].astype(jnp.float32)


def add_y(place, a, b, c, d, kept, sent):
    low = place[4]
    for q in range(4):
        for out, bit in ((kept, low), (sent, 1 - low)):
            piece = at(2 * q + bit, 384)
            out[:, q * 384 : (q + 1) * 384] = (a[:, piece] + b[:, piece]) + (c[:, piece] + d[:, piece])


def add_pair(place, a, b, *outs):
    q = place[3]
    for k, out in enumerate(outs):
        piece = at(q ^ k, 384)
        out[...] = a[:, piece] + b[:, piece]


def adam(place, a, b, c, d, state, new_state, weights):
    total = (a[...] + b[...]) + (c[...] + d[...])
    new_moment = beta_one * state[1] + (1.0 - beta_one) * total
    new_second = beta_two * state[2] + (1.0 - beta_two) * total * total
    first_hat = new_moment / (1.0 - beta_one**STEP)
    second_hat = new_second / (1.0 - beta_two**STEP)
    new_master = state[0] - learn_rate * (first_hat / (jnp.sqrt(second_hat) + adam_eps) + decay_rate * state[0])
    new_state[0] = new_master
    new_state[1] = new_moment
    new_state[2] = new_second
    weights[...] = new_master.astype(jnp.bfloat16)


def join_ring(place, *refs):
    *parts, out = refs
    width = parts[0].shape[1]
    here = place[3] if width == 384 else place[1]
    for k, part in enumerate(parts):
        out[:, at(here ^ k, width)] = part[...]


def join_pair(place, mine, other, out):
    low = place[4]
    for q in range(4):
        piece = slice(q * 384, (q + 1) * 384)
        out[:, at(2 * q + low, 384)] = mine[:, piece]
        out[:, at(2 * q + 1 - low, 384)] = other[:, piece]


def join_rows(place, *refs):
    *parts, out = refs
    core, y = place[0], place[1]
    for k in range(NY):
        piece = at(y ^ k, 3072)
        out[half(core), piece] = parts[k][...]
        out[half(1 - core), piece] = parts[NY + k][...]


def per_device(grads, master, moment, second, inputs, out_grads):
    index = lax.axis_index("dp")
    x = lax.axis_index("mp")
    core = index % NC
    z = (index // NC) % NZ
    y = index // (NC * NZ)
    first = core == 0
    place = jnp.stack([core, y, z, z // 2, z % 2, x]).astype(jnp.int32)
    f32, bf16 = jnp.float32, jnp.bfloat16

    before = swap_x(inputs, 1)
    after = swap_x(inputs, 3)
    (lhs,) = local(turn, place, (out_grads,), [((256, 512), bf16)])

    mine, sent = halves(place, grads)
    theirs = to_core(sent)

    state = jnp.stack([master, moment, second])
    kept = lax.dynamic_slice_in_dim(state, core * 32, 32, axis=1)
    got = to_core(after_that(lax.dynamic_slice_in_dim(state, (1 - core) * 32, 32, axis=1), theirs))
    state = jnp.concatenate([jnp.where(first, kept, got), jnp.where(first, got, kept)], axis=2)

    kept, *sent = local(add_cores, place, (mine, theirs), [((32, 3072), f32)] * 4)
    got = exchange(sent, [(k, 0, 0) for k in (1, 2, 3)])
    kept, sent = local(add_y, place, (kept, *got), [((32, 1536), f32)] * 2)
    got = swap_z(sent)
    kept, *sent = local(add_pair, place, (kept, got), [((32, 384), f32)] * 4)
    got = exchange(sent, [(0, 2 * k, 0) for k in (1, 2, 3)])
    state, own = local(adam, place, (kept, *got, state), [((3, 32, 384), f32), ((32, 384), bf16)])

    got = exchange([own] * 3, [(0, 2 * k, 0) for k in (1, 2, 3)])
    (own,) = local(join_ring, place, (own, *got), [((32, 1536), bf16)])

    before, after, own = lax.optimization_barrier((before, after, own))
    near = cut(PIECES[:1], before, after)
    *near, own = lax.optimization_barrier((*near, own))
    opposites = [swap_x(near[0], 3), swap_x(near[1], 1)]

    got = swap_z(own)
    (own,) = local(join_pair, place, (own, got), [((32, 3072), bf16)])
    got = exchange([own] * 3, [(k, 0, 0) for k in (1, 2, 3)])

    near = cut(PIECES[1:], before, after)
    summed, there = near_product(PIECES[1], lhs, inputs, after, before)
    *near, got0, got1, got2, there = lax.optimization_barrier((*near, *got, there))
    opposites += [swap_x(near[0], 3), swap_x(near[1], 1)]
    parts = [own, got0, got1, got2]
    others = [to_core(part) for part in parts]
    (weights,) = local(join_rows, place, (*parts, *others), [((64, D), bf16)])

    left, right = state[:, :, :192], state[:, :, 192:]
    kept = jnp.where(first, left, right)
    got = to_core(after_that(jnp.where(first, right, left), others[0]))
    state = jnp.concatenate([jnp.where(first, kept, got), jnp.where(first, got, kept)], axis=1)
    state = [state[0], state[1], state[2]]

    weights, state[0], state[1], state[2], there = lax.optimization_barrier((weights, *state, there))
    carry = product(PIECES[0][0], 4608, lhs, inputs, after, before, *opposites[:2], None, there)
    carry = far_product(PIECES[1], lhs, summed, *opposites[2:], carry)

    return (weights, state[0], state[1], state[2], carry)


def solution(mesh):
    return jax.shard_map(
        per_device,
        mesh=mesh,
        in_specs=(
            P("dp", "mp", None),
            P("mp", "dp"),
            P("mp", "dp"),
            P("mp", "dp"),
            P(("dp", "mp"), None),
            P("dp", "mp"),
        ),
        out_specs=(P("mp", None), P("mp", "dp"), P("mp", "dp"), P("mp", "dp"), P("dp", "mp", None)),
        check_vma=False,
    )
```
